1024 devices in a mesh: grp: 64 (over x, y), row: 16 (over z, core).
Axes of the slice: x: 8, y: 8, z: 8, core: 2. Of those that a mesh axis runs over, the one named last changes fastest.
Arguments:
- features: bfloat16 [262144, 256], P(('grp', 'row')), may hold values from -6 to 6
- cotangent: bfloat16 [262144, 256], P(('grp', 'row')), may hold values from -6 to 6
- degrees: int32 [262144], P(('grp', 'row')), may hold values from 16 to 64
- tile_cols: int32 [2048, 17], P(('grp', 'row')), may hold values from 0 to 31, as said below
- tile_vals: bfloat16 [2048, 17, 128, 128], P(('grp', 'row')), may hold values from 0 to 1.5, as said below
- w_self: bfloat16 [256, 256], replicated, may hold values from -0.375 to 0.375
- w_neigh: bfloat16 [256, 256], replicated, may hold values from -0.375 to 0.375
Outputs:
- output: bfloat16 [262144, 256], P(('grp', 'row'))
- features_grad: bfloat16 [262144, 256], P(('grp', 'row'))
- w_grads: float32 [2, 256, 256], replicated
The draws below stay inside these ranges and needn't reach their ends.
Inputs may be any that keep to these rules, and one draw needn't show every extreme that they name: `tile_cols`: in each partition the listed column tiles of row tile R are R + o modulo 32 for one set of 17 distinct offsets o that contains 0 and is closed under negation modulo 32; the set is drawn for each partition. `tile_vals`: the adjacency of each partition is symmetric: the tile listed at (R, C) is the transpose of the tile listed at (C, R), and a tile with R = C is symmetric. Weights lie between 0 and 1.5.
All inputs are finite; a program needn't handle non-finite values.
Results may differ from the reference program's by a relative error of at most 0.014.
Values may be sent and summed in bfloat16 or wider, within the bound.
A program may use at most 32 MiB of HBM per device.

```python
import jax
import jax.numpy as jnp
from jax import lax

F = 256
TILE = 128
NG = 4096
CT = 32
K = 8
SLOTS = 17
NODES = 262144


def shared_offsets(key):
    groups = NODES // NG
    keys = jax.random.split(key, groups)
    perms = jax.vmap(lambda single: jax.random.permutation(single, CT // 2 - 1))(keys) + 1
    chosen = perms[:, :K].astype(jnp.int32)
    zeros = jnp.zeros((groups, 1), jnp.int32)
    return jnp.concatenate([zeros, chosen, CT - chosen], axis=1)


def column_table(offsets):
    return (jnp.arange(CT, dtype=jnp.int32)[None, :, None] + offsets[:, None, :]) % CT


def draw_tile_cols(key, part):
    offsets = shared_offsets(key)
    groups = NODES // NG
    return column_table(offsets).reshape(groups * CT, SLOTS).astype(jnp.int32)


def draw_tile_vals(key, part):
    offsets = shared_offsets(key)
    key = jax.random.fold_in(key, 11)
    groups = NODES // NG
    table = column_table(offsets)
    row_ids = jnp.broadcast_to(jnp.arange(CT, dtype=jnp.int32)[:, None], (CT, SLOTS))

    def one_tile(pair_id, flipped, same):
        tile_key = jax.random.fold_in(key, pair_id)
        magnitude = jax.random.uniform(tile_key, (TILE, TILE), jnp.float32, 0.5, 1.5)
        keeper = jax.random.randint(jax.random.fold_in(tile_key, 1), (TILE, TILE), 0, 2).astype(jnp.float32)
        upper = magnitude * keeper
        return jnp.where(same, 0.5 * (upper + upper.T), jnp.where(flipped, upper.T, upper))

    def one_group(group):
        cols = table[group]
        lower = jnp.minimum(row_ids, cols)
        higher = jnp.maximum(row_ids, cols)
        pair_ids = (group * CT + lower) * CT + higher
        return jax.vmap(jax.vmap(one_tile))(pair_ids, row_ids > cols, row_ids == cols)
    values = lax.map(one_group, jnp.arange(groups, dtype=jnp.int32))
    return values.reshape(groups * CT, SLOTS, TILE, TILE).astype(jnp.bfloat16)


def with_ends(entries, own_key, smallest, top_value):
    longest = entries.shape.index(max(entries.shape))
    spots = []
    for shift in (0, 1):
        where = [jax.random.randint(jax.random.fold_in(own_key, axis), (), 0, length) for axis, length in enumerate(entries.shape)]
        where[longest] = (where[longest] + shift) % entries.shape[longest]
        spots.append(tuple(where))
    return entries.at[spots[0]].set(smallest).at[spots[1]].set(top_value)


def block_levels(stream_key, extent, cuts, least, largest):
    factor_of, own = 1.0, jax.random.fold_in(stream_key, 6)
    for axis_at, blocks in cuts:
        steps = jnp.exp(jax.random.uniform(jax.random.fold_in(own, axis_at), (blocks,), jnp.float32, least / len(cuts), largest / len(cuts)))
        factor_of = factor_of * jnp.repeat(steps, extent[axis_at] // blocks).reshape([-1 if axis == axis_at else 1 for axis in range(len(extent))])
    return factor_of


def scatter_about(stream_key, dims, width, reach, cuts=(), kind=jnp.bfloat16):
    result = jax.random.normal(stream_key, dims, jnp.float32) * width
    if len(cuts) > 0:
        result = block_levels(stream_key, dims, cuts, -0.22, 0.18) * result
    return jnp.clip(result, min=-reach, max=reach).astype(kind)


def setup_inputs(seed: int = 0) -> dict:
    arg_keys = jax.random.split(jax.random.key(seed), 8)
    features = scatter_about(arg_keys[0], (NODES, F), 1.0, 6.0, ((0, 1024),))
    cotangent = scatter_about(arg_keys[1], (NODES, F), 1.0, 6.0, ((0, 1024),))
    degrees = with_ends(jax.random.randint(arg_keys[2], (NODES,), 16, 65), jax.random.fold_in(arg_keys[2], 1), 16, 64).astype(jnp.int32)
    tile_cols = draw_tile_cols(jax.random.fold_in(arg_keys[7], 71), 0)
    tile_vals = draw_tile_vals(jax.random.fold_in(arg_keys[7], 71), 0)
    w_self = scatter_about(arg_keys[5], (F, F), F ** -0.5, 0.375)
    w_neigh = scatter_about(arg_keys[6], (F, F), F ** -0.5, 0.375)
    return {"features": features, "cotangent": cotangent, "degrees": degrees, "tile_cols": tile_cols, "tile_vals": tile_vals, "w_self": w_self, "w_neigh": w_neigh}


def partition_pass(w_self, w_neigh, items):
    feats, cotan, degs, cols, vals = items
    inverse = 1.0 / degs.astype(jnp.float32)
    blocks = feats.reshape(CT, TILE, F)
    picked = blocks[cols]
    summed = jnp.einsum("rsik,rskf->rif", vals.astype(jnp.float32), picked.astype(jnp.float32))
    aggregate = (summed.reshape(NG, F) * inverse[:, None]).astype(jnp.bfloat16)
    pre_act = jnp.dot(feats, w_self, preferred_element_type=jnp.float32) + jnp.dot(aggregate, w_neigh, preferred_element_type=jnp.float32)
    output = jax.nn.silu(pre_act).astype(jnp.bfloat16)
    sigmoid_z = jax.nn.sigmoid(pre_act)
    grad_pre = (cotan.astype(jnp.float32) * sigmoid_z * (1.0 + pre_act * (1.0 - sigmoid_z))).astype(jnp.bfloat16)
    grad_hidden = (jnp.dot(grad_pre, w_neigh.T, preferred_element_type=jnp.float32) * inverse[:, None]).astype(jnp.bfloat16)
    terms = jnp.einsum("rsik,rif->rskf", vals.astype(jnp.float32), grad_hidden.reshape(CT, TILE, F).astype(jnp.float32))
    adjoint = jnp.zeros((CT, TILE, F), jnp.float32).at[cols.reshape(-1)].add(terms.reshape(CT * SLOTS, TILE, F))
    features_grad = (jnp.dot(grad_pre, w_self.T, preferred_element_type=jnp.float32) + adjoint.reshape(NG, F)).astype(jnp.bfloat16)
    first = jnp.dot(feats.T, grad_pre, preferred_element_type=jnp.float32)
    second = jnp.dot(aggregate.T, grad_pre, preferred_element_type=jnp.float32)
    return output, features_grad, jnp.stack([first, second])


def reference(features, cotangent, degrees, tile_cols, tile_vals, w_self, w_neigh):
    groups = NODES // NG
    items = (features.reshape(groups, NG, F), cotangent.reshape(groups, NG, F), degrees.reshape(groups, NG), tile_cols.reshape(groups, CT, SLOTS), tile_vals.reshape(groups, CT, SLOTS, TILE, TILE))
    outputs, grads, partials = lax.map(lambda item: partition_pass(w_self, w_neigh, item), items)
    w_grads = jnp.sum(partials, axis=0) * (float(NODES) ** -0.5)
    return outputs.reshape(NODES, F), grads.reshape(NODES, F), w_grads
```

```python
import functools

import jax
import jax.numpy as jnp
from jax import lax
from jax.experimental import pallas as pl
from jax.experimental.pallas import tpu as pltpu
from jax.sharding import PartitionSpec as P

MESH = pl.DeviceIdType.MESH
BF16 = jnp.bfloat16
F32 = jnp.float32
CORES = 2
CHUNKS = 4


def matmul(left, right):
    return jnp.dot(left, right, preferred_element_type=F32)


def matmul_nt(left, right):
    return lax.dot_general(left, right, (((1,), (1,)), ((), ())), preferred_element_type=F32)


def matmul_tn(left, right):
    return lax.dot_general(left, right, (((0,), (0,)), ((), ())), preferred_element_type=F32)


def layer_kernel(
    side, depth, scale,
    cols, feat, cot, deg, vals, w_self, w_neigh,
    out, fgrad, wgrad,
    feats_all, hidden_all, adj, vals_v, cot_v, deg_v, ws_v, wn_v,
    inv, acc, base, left, gp, out_v, fg_v, wg_v,
    pair_out, pair_in, keep, s1, r1, s2, r2, rz, r4, r5, r6,
    in_sem, out_sem, ring1, ring2, sib1, sib2, ag_send, ar_send, ar_recv,
):
    rows, width = left.shape[1:]
    tile = vals_v.shape[2]
    slots = vals_v.shape[1]
    per_dev = rows // tile
    devs = depth * CORES
    half = depth // 2
    chunk = rows // CHUNKS
    piece = width // side
    tiles2 = s2.shape[1]

    grp, row = lax.axis_index("grp"), lax.axis_index("row")
    gx, gy = lax.div(grp, side), lax.rem(grp, side)
    z, core = lax.div(row, CORES), lax.rem(row, CORES)
    other = 1 - core
    first = (1 - core) * gx + core * gy
    second = (1 - core) * gy + core * gx

    def on_first(p):
        return ((1 - core) * (p * side + gy) + core * (gx * side + p), row)

    def on_second(p):
        return ((1 - core) * (gx * side + p) + core * (p * side + gy), row)

    def on_z(p):
        return (grp, p * CORES + core)

    sibling = (grp, z * CORES + other)

    ins = [
        pltpu.make_async_copy(feat, feats_all.at[row], in_sem.at[0]),
        pltpu.make_async_copy(vals, vals_v, in_sem.at[1]),
        pltpu.make_async_copy(deg, deg_v, in_sem.at[2]),
        pltpu.make_async_copy(w_self, ws_v, in_sem.at[3]),
        pltpu.make_async_copy(w_neigh, wn_v, in_sem.at[4]),
        pltpu.make_async_copy(cot, cot_v, in_sem.at[5]),
    ]
    for copy in ins:
        copy.start()

    barrier = pltpu.get_barrier_semaphore()
    pl.semaphore_signal(barrier, inc=1, device_id=sibling, device_id_type=MESH)

    def greet_z(i, _):
        pl.semaphore_signal(barrier, inc=1, device_id=on_z(lax.rem(z + i, depth)), device_id_type=MESH)
        return 0

    def greet_plane(i, _):
        pl.semaphore_signal(barrier, inc=1, device_id=on_first(lax.rem(first + i, side)), device_id_type=MESH)
        pl.semaphore_signal(barrier, inc=1, device_id=on_second(lax.rem(second + i, side)), device_id_type=MESH)
        return 0

    lax.fori_loop(1, depth, greet_z, 0)
    lax.fori_loop(1, side, greet_plane, 0)
    pl.semaphore_wait(barrier, depth + 2 * (side - 1))

    def owner(q):
        return lax.rem(z - q + depth, depth)

    def ring_copy(buf, recv, way, hop, q, k):
        ref = buf.at[owner(q) * CORES + core, pl.ds(k * chunk, chunk)]
        to = lax.rem(z + 1, depth) if way == 0 else lax.rem(z + depth - 1, depth)
        return pltpu.make_async_remote_copy(
            src_ref=ref, dst_ref=ref, send_sem=ag_send.at[1 if recv is ring2 else 0],
            recv_sem=recv.at[way, hop - 1, k], device_id=on_z(to), device_id_type=MESH)

    def sib_copy(buf, recv, which, q, k):
        ref = buf.at[owner(q) * CORES + core, pl.ds(k * chunk, chunk)]
        return pltpu.make_async_remote_copy(
            src_ref=ref, dst_ref=ref, send_sem=ag_send.at[which],
            recv_sem=recv.at[q], device_id=sibling, device_id_type=MESH)

    def launch(buf, recv, sib, which, k):
        ring_copy(buf, recv, 0, 1, 0, k).start()
        ring_copy(buf, recv, 1, 1, 0, k).start()
        sib_copy(buf, sib, which, 0, k).start()

    def hops(buf, recv, sib, which, hop, k0, k1):
        mid = CHUNKS // 2

        def one(way, k, onward):
            q = hop if way == 0 else depth - hop
            ring_copy(buf, recv, way, hop, q, k).wait_recv()
            if onward:
                ring_copy(buf, recv, way, hop + 1, q, k).start()
            sib_copy(buf, sib, which, q, k).start()

        if hop < half - 1:
            def both(k, _):
                one(0, k, True)
                one(1, k, True)
                return 0
            lax.fori_loop(k0, k1, both, 0)
        elif hop == half - 1:
            for k in range(k0, k1):
                one(0, k, k < mid)
                one(1, k, k >= mid)
        else:
            for k in range(k0, min(k1, mid)):
                one(0, k, False)
                one(1, k + mid, False)

    def sib_wait(buf, sib, which, q):
        block = buf.at[owner(q) * CORES + other]
        pltpu.make_async_remote_copy(
            src_ref=block, dst_ref=block, send_sem=ag_send.at[which],
            recv_sem=sib.at[q], device_id=sibling, device_id_type=MESH).wait_recv()

    def sent(buf, which):
        blocks = buf.at[pl.ds(0, 2 * depth - 1)]
        pltpu.make_async_remote_copy(
            src_ref=blocks, dst_ref=blocks, send_sem=ag_send.at[which],
            recv_sem=sib1.at[0], device_id=sibling, device_id_type=MESH).wait_send()

    def add(buf, q, who):
        b = owner(q) * CORES + who
        acc[...] += matmul(adj[b], buf[b])

    def qs(hop):
        return [0] if hop == 0 else [hop] if hop == half else [hop, depth - hop]

    ins[0].wait()
    for k in range(CHUNKS):
        launch(feats_all, ring1, sib1, 0, k)

    ins[1].wait()

    def build(b, _):
        for i in range(per_dev):
            for j in range(per_dev):
                col = b * per_dev + j
                slot, hit = 0, 0
                for s in range(slots):
                    same = cols[i, s] == col
                    slot = jnp.where(same, s, slot)
                    hit = jnp.where(same, 1, hit)
                adj[b, pl.ds(i * tile, tile), pl.ds(j * tile, tile)] = (
                    vals_v[i, slot] * jnp.float32(hit).astype(BF16))
        return 0

    lax.fori_loop(0, devs, build, 0)

    for copy in ins[2:]:
        copy.wait()
    for i in range(per_dev):
        line = 1.0 / deg_v[pl.ds(i, 1), :].astype(F32)
        square = jnp.transpose(jnp.broadcast_to(line, (tile, tile)))
        for j in range(width // tile):
            inv[pl.ds(i * tile, tile), pl.ds(j * tile, tile)] = square

    left[0] = feats_all[row]
    base[...] = matmul(left[0], ws_v[...])
    acc[...] = matmul(adj[row], left[0])

    for hop in range(1, half + 1):
        hops(feats_all, ring1, sib1, 0, hop, 0, CHUNKS)
        for q in qs(hop - 1):
            sib_wait(feats_all, sib1, 0, q)
            add(feats_all, q, other)
        for q in qs(hop):
            add(feats_all, q, core)
    sib_wait(feats_all, sib1, 0, half)
    add(feats_all, half, other)

    left[1] = (acc[...] * inv[...]).astype(BF16)
    base[...] += matmul(left[1], wn_v[...])
    pre = base[...]
    sig = jax.nn.sigmoid(pre)
    gp[...] = (cot_v[...].astype(F32) * sig * (1.0 + pre * (1.0 - sig))).astype(BF16)
    hidden_all[row] = (matmul_nt(gp[...], wn_v[...]) * inv[...]).astype(BF16)
    for k in range(CHUNKS):
        launch(hidden_all, ring2, sib2, 1, k)

    def spread(src, dst, stage, peer, me, count):
        def send(i, _):
            p = lax.rem(me + i, count)
            pltpu.make_async_remote_copy(
                src_ref=src(p), dst_ref=dst.at[me], send_sem=ar_send.at[stage],
                recv_sem=ar_recv.at[stage], device_id=peer(p), device_id_type=MESH).start()
            return 0
        lax.fori_loop(1, count, send, 0)

    def arrived(dst, stage, count):
        ref = dst.at[pl.ds(0, count - 1)]
        copy = pltpu.make_async_remote_copy(
            src_ref=ref, dst_ref=ref, send_sem=ar_send.at[stage],
            recv_sem=ar_recv.at[stage], device_id=sibling, device_id_type=MESH)
        copy.wait_recv()

    def left_here(dst, stage, count):
        ref = dst.at[pl.ds(0, count - 1)]
        pltpu.make_async_remote_copy(
            src_ref=ref, dst_ref=ref, send_sem=ar_send.at[stage],
            recv_sem=ar_recv.at[stage], device_id=sibling, device_id_type=MESH).wait_send()

    pair = pltpu.make_async_remote_copy(
        src_ref=pair_out, dst_ref=pair_in, send_sem=ar_send.at[0],
        recv_sem=ar_recv.at[0], device_id=sibling, device_id_type=MESH)
    swap = pltpu.make_async_remote_copy(
        src_ref=r5, dst_ref=r6, send_sem=ar_send.at[6],
        recv_sem=ar_recv.at[6], device_id=sibling, device_id_type=MESH)

    def stage0():
        pair_out[...] = matmul_tn(left[other], gp[...]).astype(BF16)
        pair.start()
        keep[...] = matmul_tn(left[core], gp[...])

    def stage1():
        pair.wait_recv()
        for p in range(side):
            part = pl.ds(p * piece, piece)
            s1[p] = (keep[part, :] + pair_in[part, :].astype(F32)).astype(BF16)
        spread(lambda p: s1.at[p], r1, 1, on_first, first, side)
        r1[first] = s1[first]

    def stage2():
        arrived(r1, 1, side)
        total = r1[0].astype(F32)
        for p in range(1, side):
            total += r1[p].astype(F32)
        n = 0
        for i in range(piece // 8):
            for j in range(width // 128):
                s2[n // tiles2, n % tiles2] = total[i * 8:(i + 1) * 8, j * 128:(j + 1) * 128]
                n += 1
        spread(lambda p: s2.at[p], r2, 2, on_second, second, side)
        r2[second] = s2[second]

    def stage3():
        arrived(r2, 2, side)
        total = r2[0]
        for p in range(1, side):
            total += r2[p]
        rz[z] = total
        spread(lambda p: rz.at[z], rz, 3, on_z, z, depth)

    def stage4():
        arrived(rz, 3, depth)
        total = rz[0]
        for p in range(1, depth):
            total += rz[p]
        r4[second] = total * scale
        spread(lambda p: r4.at[second], r4, 4, on_second, second, side)

    def stage5():
        arrived(r4, 4, side)
        n = 0
        for i in range(piece // 8):
            for j in range(width // 128):
                keep[i * 8:(i + 1) * 8, j * 128:(j + 1) * 128] = r4[n // tiles2, n % tiles2]
                n += 1
        r5[first] = keep[0:piece, :].astype(BF16)
        spread(lambda p: r5.at[first], r5, 5, on_first, first, side)

    def stage6():
        arrived(r5, 5, side)
        swap.start()
        for p in range(side):
            wg_v[core, pl.ds(p * piece, piece), :] = r5[p].astype(F32)

    def stage7():
        swap.wait_recv()
        for p in range(side):
            wg_v[other, pl.ds(p * piece, piece), :] = r6[p].astype(F32)

    stage0()
    out_v[...] = (pre * sig).astype(BF16)
    write_out = pltpu.make_async_copy(out_v, out, out_sem.at[0])
    write_out.start()
    acc[...] = matmul_nt(gp[...], ws_v[...])

    step = functools.partial(hops, hidden_all, ring2, sib2, 1)
    stage_after = {(1, 1): stage1, (2, 1): stage2, (2, 3): stage3, (3, 3): stage4, (half, 1): stage5}
    order = [stage1, stage2, stage3, stage4, stage5]
    for hop in range(1, half + 1):
        for k in range(CHUNKS if hop < half else CHUNKS // 2):
            step(hop, k, k + 1)
            if order and stage_after.get((hop, k)) is order[0]:
                order.pop(0)()
        if hop == 1:
            add(hidden_all, 0, core)
        for q in qs(hop - 1):
            sib_wait(hidden_all, sib2, 1, q)
            add(hidden_all, q, other)
        for q in qs(hop):
            add(hidden_all, q, core)
    for stage in order:
        stage()
    sib_wait(hidden_all, sib2, 1, half)
    add(hidden_all, half, other)
    fg_v[...] = acc[...].astype(BF16)
    write_fg = pltpu.make_async_copy(fg_v, fgrad, out_sem.at[1])
    write_fg.start()

    stage6()
    sent(feats_all, 0)
    sent(hidden_all, 1)
    pair.wait_send()
    for buf, stage, count in ((s1, 1, side), (s2, 2, side), (rz, 3, depth), (r4, 4, side), (r5, 5, side)):
        left_here(buf, stage, count)
    stage7()
    write_wg = pltpu.make_async_copy(wg_v, wgrad, out_sem.at[2])
    write_wg.start()
    swap.wait_send()
    write_out.wait()
    write_fg.wait()
    write_wg.wait()


def solution(mesh):
    groups, devs = mesh.shape["grp"], mesh.shape["row"]
    depth = devs // CORES
    side = 1
    while side * side < groups:
        side += 1
    half = depth // 2

    def shards(features, cotangent, degrees, tile_cols, tile_vals, w_self, w_neigh):
        rows, width = features.shape
        row_tiles, slots, tile, _ = tile_vals.shape
        scale = float(rows * devs * groups) ** (-0.5)
        piece = width // side
        tiles2 = piece * width // (8 * 128) // side
        block = (rows, width)
        dma = pltpu.SemaphoreType.DMA
        any_spec = pl.BlockSpec(memory_space=pl.ANY)
        return pl.pallas_call(
            functools.partial(layer_kernel, side, depth, scale),
            out_shape=(
                jax.ShapeDtypeStruct(block, BF16),
                jax.ShapeDtypeStruct(block, BF16),
                jax.ShapeDtypeStruct((2, width, width), F32),
            ),
            in_specs=[pl.BlockSpec(memory_space=pltpu.SMEM)] + [any_spec] * 6,
            out_specs=(any_spec,) * 3,
            scratch_shapes=[
                pltpu.VMEM((devs,) + block, BF16),
                pltpu.VMEM((devs,) + block, BF16),
                pltpu.VMEM((devs, rows, rows), BF16),
                pltpu.VMEM(tile_vals.shape, BF16),
                pltpu.VMEM(block, BF16),
                pltpu.VMEM((row_tiles, tile), jnp.int32),
                pltpu.VMEM((width, width), BF16),
                pltpu.VMEM((width, width), BF16),
                pltpu.VMEM(block, F32),
                pltpu.VMEM(block, F32),
                pltpu.VMEM(block, F32),
                pltpu.VMEM((2,) + block, BF16),
                pltpu.VMEM(block, BF16),
                pltpu.VMEM(block, BF16),
                pltpu.VMEM(block, BF16),
                pltpu.VMEM((2, width, width), F32),
                pltpu.VMEM((width, width), BF16),
                pltpu.VMEM((width, width), BF16),
                pltpu.VMEM((width, width), F32),
                pltpu.VMEM((side, piece, width), BF16),
                pltpu.VMEM((side, piece, width), BF16),
                pltpu.VMEM((side, tiles2, 8, 128), F32),
                pltpu.VMEM((side, tiles2, 8, 128), F32),
                pltpu.VMEM((depth, tiles2, 8, 128), F32),
                pltpu.VMEM((side, tiles2, 8, 128), F32),
                pltpu.VMEM((side, piece, width), BF16),
                pltpu.VMEM((side, piece, width), BF16),
                dma((6,)),
                dma((3,)),
                dma((2, half, CHUNKS)),
                dma((2, half, CHUNKS)),
                dma((depth,)),
                dma((depth,)),
                dma((2,)),
                dma((7,)),
                dma((7,)),
            ],
            compiler_params=pltpu.CompilerParams(
                collective_id=0, has_side_effects=True, vmem_limit_bytes=56 * 1024 * 1024),
        )(
            tile_cols, features, cotangent, degrees.reshape(row_tiles, tile), tile_vals, w_self, w_neigh)

    return jax.shard_map(
        shards,
        mesh=mesh,
        in_specs=(
            P(("grp", "row"), None),
            P(("grp", "row"), None),
            P(("grp", "row")),
            P(("grp", "row"), None),
            P(("grp", "row"), None, None, None),
            P(),
            P(),
        ),
        out_specs=(P(("grp", "row"), None), P(("grp", "row"), None), P()),
        check_vma=False,
    )
```

```python
import functools

import jax
import jax.numpy as jnp
from jax import lax
from jax.experimental import pallas as pl
from jax.experimental.pallas import tpu as pltpu
from jax.sharding import PartitionSpec as P

MESH = pl.DeviceIdType.MESH
BF16 = jnp.bfloat16
F32 = jnp.float32
CORES = 2
CHUNKS = 4


def matmul(left, right):
    return jnp.dot(left, right, preferred_element_type=F32)


def matmul_nt(left, right):
    return lax.dot_general(left, right, (((1,), (1,)), ((), ())), preferred_element_type=F32)


def matmul_tn(left, right):
    return lax.dot_general(left, right, (((0,), (0,)), ((), ())), preferred_element_type=F32)


def layer_kernel(
    side, depth, scale,
    cols_in, feat, cot, deg, vals, w_self, w_neigh,
    out, fgrad, wgrad,
    cols, feats_all, hidden_all, adj, vals_v, cot_v, deg_v, ws_v, wn_v,
    inv, acc, base, left, gp, out_v, fg_v, wg_v,
    pair_out, pair_in, keep, s1, r1, s2, r2, rz, r4, r5, r6,
    in_sem, out_sem, ring1, ring2, sib1, sib2, ag_send, ar_send, ar_recv, relay,
):
    rows, width = left.shape[1:]
    tile = vals_v.shape[2]
    slots = vals_v.shape[1]
    per_dev = rows // tile
    devs = depth * CORES
    half = depth // 2
    rounds = relay.shape[0]
    chunk = rows // CHUNKS
    piece = width // side
    tiles2 = s2.shape[1]

    grp, row = lax.axis_index("grp"), lax.axis_index("row")
    gx, gy = lax.div(grp, side), lax.rem(grp, side)
    z, core = lax.div(row, CORES), lax.rem(row, CORES)
    other = 1 - core
    first = (1 - core) * gx + core * gy
    second = (1 - core) * gy + core * gx

    def on_first(p):
        return ((1 - core) * (p * side + gy) + core * (gx * side + p), row)

    def on_second(p):
        return ((1 - core) * (gx * side + p) + core * (p * side + gy), row)

    def on_z(p):
        return (grp, p * CORES + core)

    sibling = (grp, z * CORES + other)

    ins = [
        pltpu.make_async_copy(feat, feats_all.at[row], in_sem.at[0]),
        pltpu.make_async_copy(vals, vals_v, in_sem.at[1]),
        pltpu.make_async_copy(deg, deg_v, in_sem.at[2]),
        pltpu.make_async_copy(w_self, ws_v, in_sem.at[3]),
        pltpu.make_async_copy(w_neigh, wn_v, in_sem.at[4]),
        pltpu.make_async_copy(cot, cot_v, in_sem.at[5]),
        pltpu.make_async_copy(cols_in, cols, in_sem.at[6]),
    ]
    for copy in ins:
        copy.start()

    barrier = pltpu.get_barrier_semaphore()
    up, down = lax.rem(z + 1, depth), lax.rem(z + depth - 1, depth)
    around = [
        on_first(lax.rem(first + 1, side)), on_first(lax.rem(first + side - 1, side)),
        on_second(lax.rem(second + 1, side)), on_second(lax.rem(second + side - 1, side)),
    ]
    for device in [on_z(up), on_z(down), sibling] + around:
        pl.semaphore_signal(barrier, inc=1, device_id=device, device_id_type=MESH)
    pl.semaphore_wait(barrier, 3 + len(around))

    def relay_send(i):
        for device in around:
            pl.semaphore_signal(relay.at[i], inc=1, device_id=device, device_id_type=MESH)

    def relay_wait(i):
        pl.semaphore_wait(relay.at[i], len(around))

    def owner(q):
        return lax.rem(z - q + depth, depth)

    def ring_copy(buf, recv, way, hop, q, k, src=None):
        ref = buf.at[owner(q) * CORES + core, pl.ds(k * chunk, chunk)]
        to = up if way == 0 else down
        return pltpu.make_async_remote_copy(
            src_ref=ref if src is None else src, dst_ref=ref, send_sem=ag_send.at[1 if recv is ring2 else 0],
            recv_sem=recv.at[way, hop - 1, k], device_id=on_z(to), device_id_type=MESH)

    def sib_copy(buf, recv, which, q, k, src=None):
        ref = buf.at[owner(q) * CORES + core, pl.ds(k * chunk, chunk)]
        return pltpu.make_async_remote_copy(
            src_ref=ref if src is None else src, dst_ref=ref, send_sem=ag_send.at[which],
            recv_sem=recv.at[q], device_id=sibling, device_id_type=MESH)

    def launch(buf, recv, sib, which, origin):
        for k in range(CHUNKS):
            src = origin.at[pl.ds(k * chunk, chunk)]
            ring_copy(buf, recv, 0, 1, 0, k, src).start()
            ring_copy(buf, recv, 1, 1, 0, k, src).start()
        for k in range(CHUNKS):
            sib_copy(buf, sib, which, 0, k, origin.at[pl.ds(k * chunk, chunk)]).start()

    def hops(buf, recv, sib, which, hop, k0, k1):
        mid = CHUNKS // 2

        def one(way, k, onward):
            q = hop if way == 0 else depth - hop
            ring_copy(buf, recv, way, hop, q, k).wait_recv()
            if onward:
                ring_copy(buf, recv, way, hop + 1, q, k).start()
            sib_copy(buf, sib, which, q, k).start()

        if hop < half - 1:
            def both(k, _):
                one(0, k, True)
                one(1, k, True)
                return 0
            lax.fori_loop(k0, k1, both, 0)
        elif hop == half - 1:
            for k in range(k0, k1):
                one(0, k, k < mid)
                one(1, k, k >= mid)
        else:
            for k in range(k0, min(k1, mid)):
                one(0, k, False)
                one(1, k + mid, False)

    def sib_wait(buf, sib, which, q):
        block = buf.at[owner(q) * CORES + other]
        pltpu.make_async_remote_copy(
            src_ref=block, dst_ref=block, send_sem=ag_send.at[which],
            recv_sem=sib.at[q], device_id=sibling, device_id_type=MESH).wait_recv()

    def sent(buf, which):
        blocks = buf.at[pl.ds(0, 2 * depth - 1)]
        pltpu.make_async_remote_copy(
            src_ref=blocks, dst_ref=blocks, send_sem=ag_send.at[which],
            recv_sem=sib1.at[0], device_id=sibling, device_id_type=MESH).wait_send()

    def add(buf, q, who):
        b = owner(q) * CORES + who
        acc[...] += matmul(adj[b], buf[b])

    def qs(hop):
        return [0] if hop == 0 else [hop] if hop == half else [hop, depth - hop]

    launch(feats_all, ring1, sib1, 0, feat)
    relay_send(0)

    ins[1].wait()
    ins[6].wait()

    def build(b, _):
        for i in range(per_dev):
            for j in range(per_dev):
                col = b * per_dev + j
                slot, hit = 0, 0
                for s in range(slots):
                    same = cols[i, s] == col
                    slot = jnp.where(same, s, slot)
                    hit = jnp.where(same, 1, hit)
                adj[b, pl.ds(i * tile, tile), pl.ds(j * tile, tile)] = (
                    vals_v[i, slot] * jnp.float32(hit).astype(BF16))
        return 0

    lax.fori_loop(0, devs, build, 0)

    for copy in ins[:1] + ins[2:6]:
        copy.wait()
    for i in range(per_dev):
        line = 1.0 / deg_v[pl.ds(i, 1), :].astype(F32)
        square = jnp.transpose(jnp.broadcast_to(line, (tile, tile)))
        for j in range(width // tile):
            inv[pl.ds(i * tile, tile), pl.ds(j * tile, tile)] = square

    left[0] = feats_all[row]
    base[...] = matmul(left[0], ws_v[...])
    acc[...] = matmul(adj[row], left[0])

    for hop in range(1, half + 1):
        hops(feats_all, ring1, sib1, 0, hop, 0, CHUNKS)
        for q in qs(hop - 1):
            sib_wait(feats_all, sib1, 0, q)
            add(feats_all, q, other)
        for q in qs(hop):
            add(feats_all, q, core)
        if hop <= rounds:
            relay_wait(hop - 1)
            if hop < rounds:
                relay_send(hop)
    for i in range(half, rounds):
        relay_wait(i)
        if i + 1 < rounds:
            relay_send(i + 1)
    sib_wait(feats_all, sib1, 0, half)
    add(feats_all, half, other)

    left[1] = (acc[...] * inv[...]).astype(BF16)
    base[...] += matmul(left[1], wn_v[...])
    pre = base[...]
    sig = jax.nn.sigmoid(pre)
    gp[...] = (cot_v[...].astype(F32) * sig * (1.0 + pre * (1.0 - sig))).astype(BF16)
    def far_first(count):
        return sorted(range(1, count), key=lambda i: (-min(i, count - i), i))

    def spread(src, dst, stage, peer, me, count):
        for i in far_first(count):
            p = lax.rem(me + i, count)
            pltpu.make_async_remote_copy(
                src_ref=src(p), dst_ref=dst.at[me], send_sem=ar_send.at[stage],
                recv_sem=ar_recv.at[stage], device_id=peer(p), device_id_type=MESH).start()

    def arrived(dst, stage, count):
        ref = dst.at[pl.ds(0, count - 1)]
        copy = pltpu.make_async_remote_copy(
            src_ref=ref, dst_ref=ref, send_sem=ar_send.at[stage],
            recv_sem=ar_recv.at[stage], device_id=sibling, device_id_type=MESH)
        copy.wait_recv()

    def left_here(dst, stage, count):
        ref = dst.at[pl.ds(0, count - 1)]
        pltpu.make_async_remote_copy(
            src_ref=ref, dst_ref=ref, send_sem=ar_send.at[stage],
            recv_sem=ar_recv.at[stage], device_id=sibling, device_id_type=MESH).wait_send()

    pair = pltpu.make_async_remote_copy(
        src_ref=pair_out, dst_ref=pair_in, send_sem=ar_send.at[0],
        recv_sem=ar_recv.at[0], device_id=sibling, device_id_type=MESH)
    swap = pltpu.make_async_remote_copy(
        src_ref=r5, dst_ref=r6, send_sem=ar_send.at[6],
        recv_sem=ar_recv.at[6], device_id=sibling, device_id_type=MESH)

    def stage0():
        pair_out[...] = matmul_tn(left[other], gp[...]).astype(BF16)
        pair.start()
        hidden_all[row] = (matmul_nt(gp[...], wn_v[...]) * inv[...]).astype(BF16)
        launch(hidden_all, ring2, sib2, 1, hidden_all.at[row])
        keep[...] = matmul_tn(left[core], gp[...])

    def stage1():
        pair.wait_recv()

        def ready(p):
            part = pl.ds(pl.multiple_of(p * piece, piece), piece)
            s1[p] = (keep[part, :] + pair_in[part, :].astype(F32)).astype(BF16)
            return s1.at[p]

        spread(ready, r1, 1, on_first, first, side)
        r1[first] = ready(first)[...]

    def stage2():
        arrived(r1, 1, side)
        total = r1[0].astype(F32)
        for p in range(1, side):
            total += r1[p].astype(F32)
        n = 0
        for i in range(piece // 8):
            for j in range(width // 128):
                s2[n // tiles2, n % tiles2] = total[i * 8:(i + 1) * 8, j * 128:(j + 1) * 128]
                n += 1
        spread(lambda p: s2.at[p], r2, 2, on_second, second, side)
        r2[second] = s2[second]

    def stage3():
        arrived(r2, 2, side)
        total = r2[0]
        for p in range(1, side):
            total += r2[p]
        rz[z] = total
        spread(lambda p: rz.at[z], rz, 3, on_z, z, depth)

    def stage4():
        arrived(rz, 3, depth)
        total = rz[0]
        for p in range(1, depth):
            total += rz[p]
        r4[second] = total * scale
        spread(lambda p: r4.at[second], r4, 4, on_second, second, side)

    def stage5():
        arrived(r4, 4, side)
        n = 0
        for i in range(piece // 8):
            for j in range(width // 128):
                keep[i * 8:(i + 1) * 8, j * 128:(j + 1) * 128] = r4[n // tiles2, n % tiles2]
                n += 1
        r5[first] = keep[0:piece, :].astype(BF16)
        spread(lambda p: r5.at[first], r5, 5, on_first, first, side)

    def stage6():
        arrived(r5, 5, side)
        swap.start()
        for p in range(side):
            wg_v[core, pl.ds(p * piece, piece), :] = r5[p].astype(F32)

    def stage7():
        swap.wait_recv()
        for p in range(side):
            wg_v[other, pl.ds(p * piece, piece), :] = r6[p].astype(F32)

    stage0()
    out_v[...] = (pre * sig).astype(BF16)
    write_out = pltpu.make_async_copy(out_v, out, out_sem.at[0])
    write_out.start()
    acc[...] = matmul_nt(gp[...], ws_v[...])

    stage1()
    for hop, stage in zip(range(1, half + 1), [stage2, stage3, stage4] + [None] * half):
        hops(hidden_all, ring2, sib2, 1, hop, 0, CHUNKS)
        if stage is not None and hop < half:
            stage()
        if hop == 1:
            add(hidden_all, 0, core)
        for q in qs(hop - 1):
            sib_wait(hidden_all, sib2, 1, q)
            add(hidden_all, q, other)
        for q in qs(hop):
            add(hidden_all, q, core)
    for stage in [stage2, stage3, stage4][half - 1:]:
        stage()
    sib_wait(hidden_all, sib2, 1, half)
    add(hidden_all, half, other)
    fg_v[...] = acc[...].astype(BF16)
    write_fg = pltpu.make_async_copy(fg_v, fgrad, out_sem.at[1])
    write_fg.start()

    stage5()
    stage6()
    sent(feats_all, 0)
    sent(hidden_all, 1)
    pair.wait_send()
    for buf, stage, count in ((s1, 1, side), (s2, 2, side), (rz, 3, depth), (r4, 4, side), (r5, 5, side)):
        left_here(buf, stage, count)
    stage7()
    write_wg = pltpu.make_async_copy(wg_v, wgrad, out_sem.at[2])
    write_wg.start()
    swap.wait_send()
    write_out.wait()
    write_fg.wait()
    write_wg.wait()


def deliver(out_in, fgrad_in, wgrad_in, out, fgrad, wgrad, sem):
    copies = [
        pltpu.make_async_copy(src, dst, sem.at[i])
        for i, (src, dst) in enumerate([(out_in, out), (fgrad_in, fgrad), (wgrad_in, wgrad)])
    ]
    for copy in copies:
        copy.start()
    for copy in copies:
        copy.wait()


def solution(mesh):
    groups, devs = mesh.shape["grp"], mesh.shape["row"]
    depth = devs // CORES
    side = 1
    while side * side < groups:
        side += 1
    half = depth // 2

    def shards(features, cotangent, degrees, tile_cols, tile_vals, w_self, w_neigh):
        rows, width = features.shape
        row_tiles, slots, tile, _ = tile_vals.shape
        scale = float(rows * devs * groups) ** (-0.5)
        piece = width // side
        tiles2 = piece * width // (8 * 128) // side
        block = (rows, width)
        dma = pltpu.SemaphoreType.DMA
        any_spec = pl.BlockSpec(memory_space=pl.ANY)
        hbm = pl.BlockSpec(memory_space=pltpu.HBM)
        results = pl.pallas_call(
            functools.partial(layer_kernel, side, depth, scale),
            out_shape=(
                jax.ShapeDtypeStruct(block, BF16),
                jax.ShapeDtypeStruct(block, BF16),
                jax.ShapeDtypeStruct((2, width, width), F32),
            ),
            in_specs=[hbm] * 7,
            out_specs=(pl.BlockSpec(memory_space=pltpu.VMEM),) * 3,
            scratch_shapes=[
                pltpu.SMEM(tile_cols.shape, jnp.int32),
                pltpu.VMEM((devs,) + block, BF16),
                pltpu.VMEM((devs,) + block, BF16),
                pltpu.VMEM((devs, rows, rows), BF16),
                pltpu.VMEM(tile_vals.shape, BF16),
                pltpu.VMEM(block, BF16),
                pltpu.VMEM((row_tiles, tile), jnp.int32),
                pltpu.VMEM((width, width), BF16),
                pltpu.VMEM((width, width), BF16),
                pltpu.VMEM(block, F32),
                pltpu.VMEM(block, F32),
                pltpu.VMEM(block, F32),
                pltpu.VMEM((2,) + block, BF16),
                pltpu.VMEM(block, BF16),
                pltpu.VMEM(block, BF16),
                pltpu.VMEM(block, BF16),
                pltpu.VMEM((2, width, width), F32),
                pltpu.VMEM((width, width), BF16),
                pltpu.VMEM((width, width), BF16),
                pltpu.VMEM((width, width), F32),
                pltpu.VMEM((side, piece, width), BF16),
                pltpu.VMEM((side, piece, width), BF16),
                pltpu.VMEM((side, tiles2, 8, 128), F32),
                pltpu.VMEM((side, tiles2, 8, 128), F32),
                pltpu.VMEM((depth, tiles2, 8, 128), F32),
                pltpu.VMEM((side, tiles2, 8, 128), F32),
                pltpu.VMEM((side, piece, width), BF16),
                pltpu.VMEM((side, piece, width), BF16),
                dma((7,)),
                dma((3,)),
                dma((2, half, CHUNKS)),
                dma((2, half, CHUNKS)),
                dma((depth,)),
                dma((depth,)),
                dma((2,)),
                dma((7,)),
                dma((7,)),
                pltpu.SemaphoreType.REGULAR((max(1, side // 2 - 1),)),
            ],
            compiler_params=pltpu.CompilerParams(
                collective_id=0, has_side_effects=True, vmem_limit_bytes=56 * 1024 * 1024),
        )(
            tile_cols, features, cotangent, degrees.reshape(row_tiles, tile), tile_vals, w_self, w_neigh)
        return pl.pallas_call(
            deliver,
            out_shape=[jax.ShapeDtypeStruct(r.shape, r.dtype) for r in results],
            in_specs=[pl.BlockSpec(memory_space=pltpu.VMEM)] * 3,
            out_specs=[hbm] * 3,
            scratch_shapes=[dma((3,))],
            compiler_params=pltpu.CompilerParams(vmem_limit_bytes=56 * 1024 * 1024),
        )(*results)

    return jax.shard_map(
        shards,
        mesh=mesh,
        in_specs=(
            P(("grp", "row"), None),
            P(("grp", "row"), None),
            P(("grp", "row")),
            P(("grp", "row"), None),
            P(("grp", "row"), None, None, None),
            P(),
            P(),
        ),
        out_specs=(P(("grp", "row"), None), P(("grp", "row"), None), P()),
        check_vma=False,
    )
```

```python
import functools

import jax
import jax.numpy as jnp
from jax import lax
from jax.experimental import pallas as pl
from jax.experimental.pallas import tpu as pltpu
from jax.sharding import PartitionSpec as P

MESH = pl.DeviceIdType.MESH
BF16 = jnp.bfloat16
F32 = jnp.float32
CORES = 2
CHUNKS = 4


def matmul(left, right):
    return jnp.dot(left, right, preferred_element_type=F32)


def matmul_nt(left, right):
    return lax.dot_general(left, right, (((1,), (1,)), ((), ())), preferred_element_type=F32)


def matmul_tn(left, right):
    return lax.dot_general(left, right, (((0,), (0,)), ((), ())), preferred_element_type=F32)


def layer_kernel(
    side, depth, scale,
    cols_in, feat, cot, deg, vals, w_self, w_neigh,
    out, fgrad, wgrad,
    cols, places_v, places, feats_all, hidden_all, adj, vals_v, cot_v, deg_v, ws_v, wn_v,
    inv, acc, base, left, gp, out_v, fg_v,
    pair_out, pair_in, keep, s1, r1, r2, r3, r5,
    in_sem, out_sem, ring, near, sib, ag_send, ar_send, ar_recv, relay,
):
    rows, width = left.shape[1:]
    tile = vals_v.shape[2]
    slots = vals_v.shape[1]
    per_dev = rows // tile
    devs = depth * CORES
    half = depth // 2
    rounds = relay.shape[0]
    chunk = rows // CHUNKS
    piece = width // side

    grp, row = lax.axis_index("grp"), lax.axis_index("row")
    gx, gy = lax.div(grp, side), lax.rem(grp, side)
    z, core = lax.div(row, CORES), lax.rem(row, CORES)
    other = 1 - core
    first = (1 - core) * gx + core * gy
    second = (1 - core) * gy + core * gx

    def on_first(p):
        return ((1 - core) * (p * side + gy) + core * (gx * side + p), row)

    def on_second(p):
        return ((1 - core) * (gx * side + p) + core * (p * side + gy), row)

    def on_z(p):
        return (grp, p * CORES + core)

    sibling = (grp, z * CORES + other)

    ins = [
        pltpu.make_async_copy(feat, feats_all.at[row], in_sem.at[0]),
        pltpu.make_async_copy(vals, vals_v, in_sem.at[1]),
        pltpu.make_async_copy(deg, deg_v, in_sem.at[2]),
        pltpu.make_async_copy(w_self, ws_v, in_sem.at[3]),
        pltpu.make_async_copy(w_neigh, wn_v, in_sem.at[4]),
        pltpu.make_async_copy(cot, cot_v, in_sem.at[5]),
        pltpu.make_async_copy(cols_in, cols, in_sem.at[6]),
    ]
    for copy in ins:
        copy.start()

    barrier = pltpu.get_barrier_semaphore()
    up, down = lax.rem(z + 1, depth), lax.rem(z + depth - 1, depth)
    around = [
        on_first(lax.rem(first + 1, side)), on_first(lax.rem(first + side - 1, side)),
        on_second(lax.rem(second + 1, side)), on_second(lax.rem(second + side - 1, side)),
    ]
    for device in [on_z(up), on_z(down), sibling] + around:
        pl.semaphore_signal(barrier, inc=1, device_id=device, device_id_type=MESH)
    pl.semaphore_wait(barrier, 3 + len(around))

    def relay_send(i):
        for device in around:
            pl.semaphore_signal(relay.at[i], inc=1, device_id=device, device_id_type=MESH)

    def relay_wait(i):
        pl.semaphore_wait(relay.at[i], len(around))

    onward = on_z(core * down + other * up)

    def chip(hop):
        return lax.rem(z + (2 * core - 1) * hop + depth, depth)

    def part(buf, hop, own, k):
        who = core if own else other
        return buf.at[chip(hop) * CORES + who, pl.ds(k * chunk, chunk)]

    def ring_copy(buf, which, hop, own, k, src=None):
        ref = part(buf, hop, own, k)
        return pltpu.make_async_remote_copy(
            src_ref=ref if src is None else src, dst_ref=ref, send_sem=ag_send.at[which],
            recv_sem=ring.at[which, 0 if own else 1, hop, k], device_id=onward, device_id_type=MESH)

    def ring_wait(buf, which, hop, own, k):
        ref = part(buf, hop, own, k)
        pltpu.make_async_remote_copy(
            src_ref=ref, dst_ref=ref, send_sem=ag_send.at[which],
            recv_sem=ring.at[which, 0 if own else 1, hop - 1, k],
            device_id=onward, device_id_type=MESH).wait_recv()

    def sib_copy(ref, which, sem, src=None):
        return pltpu.make_async_remote_copy(
            src_ref=ref if src is None else src, dst_ref=ref, send_sem=ag_send.at[which],
            recv_sem=sem, device_id=sibling, device_id_type=MESH)

    def launch_own(buf, which, origin):
        for k in range(CHUNKS):
            src = origin.at[pl.ds(k * chunk, chunk)]
            sib_copy(part(buf, 0, True, k), which, near.at[which, k], src).start()
            ring_copy(buf, which, 0, True, k, src).start()

    def launch_other(buf, which):
        def one(k, _):
            sib_copy(part(buf, 0, False, k), which, near.at[which, k]).wait_recv()
            ring_copy(buf, which, 0, False, k).start()
            return 0
        lax.fori_loop(0, CHUNKS, one, 0)

    def hop_in(buf, which, hop):
        for own in (True, False)[:2 if hop < half else 1]:
            def one(k, _):
                ring_wait(buf, which, hop, own, k)
                if hop < half - 1 or (hop == half - 1 and own):
                    ring_copy(buf, which, hop, own, k).start()
                sib_copy(part(buf, hop, own, k), which, sib.at[which, hop - 1, 0 if own else 1]).start()
                return 0
            lax.fori_loop(0, CHUNKS, one, 0)

    def sib_in(buf, which, hop):
        for i in range(2 if hop < half else 1):
            block = buf.at[0]
            sib_copy(block, which, sib.at[which, hop - 1, i]).wait_recv()

    def sent(buf, which):
        blocks = buf.at[pl.ds(0, 2 * depth - 1)]
        sib_copy(blocks, which, near.at[which, 0]).wait_send()

    def add(buf, hop):
        at = chip(hop)
        acc[...] += matmul(adj[at], buf[pl.ds(CORES * at, CORES)].reshape(CORES * rows, width))

    launch_own(feats_all, 0, feat)
    relay_send(0)
    launch_other(feats_all, 0)

    ins[6].wait()
    lane = lax.broadcasted_iota(jnp.int32, (per_dev, 128), 1)
    place, listed = jnp.zeros_like(lane), jnp.zeros_like(lane)
    for s in range(slots):
        same = cols[:, s:s + 1] == lane
        place = jnp.where(same, s, place)
        listed = jnp.where(same, 1, listed)
    places_v[0:per_dev, :] = place
    places_v[per_dev:2 * per_dev, :] = listed
    to_scalar = pltpu.make_async_copy(places_v, places, in_sem.at[7])
    to_scalar.start()
    ins[1].wait()
    to_scalar.wait()

    def build(hop):
        at = chip(hop)
        for i in range(per_dev):
            for j in range(CORES * per_dev):
                col = at * (CORES * per_dev) + j
                listed = places[per_dev + i, col]
                adj[at, pl.ds(i * tile, tile), pl.ds(j * tile, tile)] = (
                    vals_v[i, places[i, col]] * jnp.float32(listed).astype(BF16))

    build(0)
    for copy in ins[:1] + ins[2:6]:
        copy.wait()
    for i in range(per_dev):
        line = 1.0 / deg_v[pl.ds(i, 1), :].astype(F32)
        square = jnp.transpose(jnp.broadcast_to(line, (tile, tile)))
        for j in range(width // tile):
            inv[pl.ds(i * tile, tile), pl.ds(j * tile, tile)] = square

    left[0] = feats_all[row]
    base[...] = matmul(left[0], ws_v[...])
    acc[...] = jnp.zeros_like(acc)
    add(feats_all, 0)
    for hop in range(1, half + 1):
        hop_in(feats_all, 0, hop)
        build(hop)
        if hop < half:
            build(-hop)
            add(feats_all, hop)
        if 1 < hop <= rounds + 1:
            relay_wait(hop - 2)
            if hop <= rounds:
                relay_send(hop - 1)
    for hop in range(1, half + 1):
        sib_in(feats_all, 0, hop)
        add(feats_all, -hop)
    for i in range(half - 1, rounds):
        relay_wait(i)
        if i + 1 < rounds:
            relay_send(i + 1)

    left[1] = (acc[...] * inv[...]).astype(BF16)
    base[...] += matmul(left[1], wn_v[...])
    pre = base[...]
    sig = jax.nn.sigmoid(pre)
    gp[...] = (cot_v[...].astype(F32) * sig * (1.0 + pre * (1.0 - sig))).astype(BF16)
    def far_first(count):
        return sorted(range(1, count), key=lambda i: (-min(i, count - i), i))

    def spread(src, dst, stage, peer, me, count):
        for i in far_first(count):
            p = lax.rem(me + i, count)
            pltpu.make_async_remote_copy(
                src_ref=src(p), dst_ref=dst.at[me], send_sem=ar_send.at[stage],
                recv_sem=ar_recv.at[stage], device_id=peer(p), device_id_type=MESH).start()

    def arrived(dst, stage, count):
        ref = dst.at[pl.ds(0, count - 1)]
        copy = pltpu.make_async_remote_copy(
            src_ref=ref, dst_ref=ref, send_sem=ar_send.at[stage],
            recv_sem=ar_recv.at[stage], device_id=sibling, device_id_type=MESH)
        copy.wait_recv()

    def left_here(dst, stage, count):
        ref = dst.at[pl.ds(0, count - 1)]
        pltpu.make_async_remote_copy(
            src_ref=ref, dst_ref=ref, send_sem=ar_send.at[stage],
            recv_sem=ar_recv.at[stage], device_id=sibling, device_id_type=MESH).wait_send()

    pair = pltpu.make_async_remote_copy(
        src_ref=pair_out, dst_ref=pair_in, send_sem=ar_send.at[0],
        recv_sem=ar_recv.at[0], device_id=sibling, device_id_type=MESH)
    swap = pltpu.make_async_remote_copy(
        src_ref=r5, dst_ref=wgrad.at[core], send_sem=ar_send.at[6],
        recv_sem=ar_recv.at[6], device_id=sibling, device_id_type=MESH)

    write_wg = pltpu.make_async_copy(r5, wgrad.at[core], out_sem.at[2])

    def stage0():
        pair_out[...] = matmul_tn(left[other], gp[...]).astype(BF16)
        pair.start()
        hidden_all[row] = (matmul_nt(gp[...], wn_v[...]) * inv[...]).astype(BF16)
        launch_own(hidden_all, 1, hidden_all.at[row])
        keep[...] = matmul_tn(left[core], gp[...])

    def stage1():
        pair.wait_recv()

        def ready(p):
            part = pl.ds(pl.multiple_of(p * piece, piece), piece)
            s1[p] = (keep[part, :] + pair_in[part, :].astype(F32)).astype(BF16)
            return s1.at[p]

        spread(ready, r1, 1, on_first, first, side)
        r1[first] = ready(first)[...]

    z_early = core if side == depth else 0

    def on_cross(by_z, p):
        across, along = on_second(p), on_z(p)
        return tuple(by_z * a + (1 - by_z) * b for a, b in zip(along, across))

    def total(ref, count):
        value = ref[0].astype(F32)
        for p in range(1, count):
            value += ref[p].astype(F32)
        return value

    def cross(by_z, dst, stage, count, value):
        me = by_z * z + (1 - by_z) * second
        dst[me] = value.astype(BF16)
        spread(lambda p: dst.at[me], dst, stage, functools.partial(on_cross, by_z), me, count)

    def stage2():
        arrived(r1, 1, side)
        cross(z_early, r2, 2, side, total(r1, side))

    def stage3():
        arrived(r2, 2, side)
        cross(1 - z_early, r3, 3, depth, total(r2, side))

    def stage5():
        arrived(r3, 3, depth)
        r5[first] = (total(r3, depth) * scale).astype(BF16)
        spread(lambda p: r5.at[first], r5, 5, on_first, first, side)

    def stage6():
        arrived(r5, 5, side)
        swap.start()
        write_wg.start()

    stage0()
    stage1()
    launch_other(hidden_all, 1)
    out_v[...] = (pre * sig).astype(BF16)
    write_out = pltpu.make_async_copy(out_v, out, out_sem.at[0])
    write_out.start()
    acc[...] = matmul_nt(gp[...], ws_v[...])
    add(hidden_all, 0)
    stages = [stage2, stage3, stage5]
    for hop in range(1, half + 1):
        hop_in(hidden_all, 1, hop)
        if stages:
            stages.pop(0)()
        if hop < half:
            add(hidden_all, hop)
    for stage in stages:
        stage()
    for hop in range(1, half + 1):
        sib_in(hidden_all, 1, hop)
        add(hidden_all, -hop)
    fg_v[...] = acc[...].astype(BF16)
    write_fg = pltpu.make_async_copy(fg_v, fgrad, out_sem.at[1])
    write_fg.start()

    stage6()
    sent(feats_all, 0)
    sent(hidden_all, 1)
    pair.wait_send()
    for buf, stage, count in ((s1, 1, side), (r2, 2, side), (r3, 3, depth), (r5, 5, side)):
        left_here(buf, stage, count)
    swap.wait()
    write_out.wait()
    write_fg.wait()
    write_wg.wait()


def deliver(out_in, fgrad_in, wgrad_in, out, fgrad, wgrad):
    out[...] = out_in[...]
    fgrad[...] = fgrad_in[...]
    wgrad[...] = wgrad_in[...].astype(F32).reshape(wgrad.shape)


def solution(mesh):
    groups, devs = mesh.shape["grp"], mesh.shape["row"]
    depth = devs // CORES
    side = 1
    while side * side < groups:
        side += 1
    half = depth // 2

    def shards(features, cotangent, degrees, tile_cols, tile_vals, w_self, w_neigh):
        rows, width = features.shape
        row_tiles, slots, tile, _ = tile_vals.shape
        scale = float(rows * devs * groups) ** (-0.5)
        piece = width // side
        block = (rows, width)
        dma = pltpu.SemaphoreType.DMA
        any_spec = pl.BlockSpec(memory_space=pl.ANY)
        hbm = pl.BlockSpec(memory_space=pltpu.HBM)
        results = pl.pallas_call(
            functools.partial(layer_kernel, side, depth, scale),
            out_shape=(
                jax.ShapeDtypeStruct(block, BF16),
                jax.ShapeDtypeStruct(block, BF16),
                jax.ShapeDtypeStruct((2, side, piece, width), BF16),
            ),
            in_specs=[hbm] * 7,
            out_specs=(any_spec,) * 3,
            scratch_shapes=[
                pltpu.VMEM(tile_cols.shape, jnp.int32),
                pltpu.VMEM((2 * row_tiles, 128), jnp.int32),
                pltpu.SMEM((2 * row_tiles, 128), jnp.int32),
                pltpu.VMEM((devs,) + block, BF16),
                pltpu.VMEM((devs,) + block, BF16),
                pltpu.VMEM((depth, rows, CORES * rows), BF16),
                pltpu.VMEM(tile_vals.shape, BF16),
                pltpu.VMEM(block, BF16),
                pltpu.VMEM((row_tiles, tile), jnp.int32),
                pltpu.VMEM((width, width), BF16),
                pltpu.VMEM((width, width), BF16),
                pltpu.VMEM(block, F32),
                pltpu.VMEM(block, F32),
                pltpu.VMEM(block, F32),
                pltpu.VMEM((2,) + block, BF16),
                pltpu.VMEM(block, BF16),
                pltpu.VMEM(block, BF16),
                pltpu.VMEM(block, BF16),
                pltpu.VMEM((width, width), BF16),
                pltpu.VMEM((width, width), BF16),
                pltpu.VMEM((width, width), F32),
                pltpu.VMEM((side, piece, width), BF16),
                pltpu.VMEM((side, piece, width), BF16),
                pltpu.VMEM((side, piece, width), BF16),
                pltpu.VMEM((depth, piece, width), BF16),
                pltpu.VMEM((side, piece, width), BF16),
                dma((8,)),
                dma((3,)),
                dma((2, 2, half, CHUNKS)),
                dma((2, CHUNKS)),
                dma((2, half, 2)),
                dma((2,)),
                dma((7,)),
                dma((7,)),
                pltpu.SemaphoreType.REGULAR((max(1, side // 2 - 1),)),
            ],
            compiler_params=pltpu.CompilerParams(
                collective_id=0, has_side_effects=True, vmem_limit_bytes=56 * 1024 * 1024),
        )(
            tile_cols, features, cotangent, degrees.reshape(row_tiles, tile), tile_vals, w_self, w_neigh)
        whole = pl.BlockSpec(memory_space=pltpu.VMEM)
        return pl.pallas_call(
            deliver,
            out_shape=(
                jax.ShapeDtypeStruct(block, BF16),
                jax.ShapeDtypeStruct(block, BF16),
                jax.ShapeDtypeStruct((2, width, width), F32),
            ),
            in_specs=[whole] * 3,
            out_specs=(whole,) * 3,
            compiler_params=pltpu.CompilerParams(vmem_limit_bytes=56 * 1024 * 1024),
        )(*results)

    return jax.shard_map(
        shards,
        mesh=mesh,
        in_specs=(
            P(("grp", "row"), None),
            P(("grp", "row"), None),
            P(("grp", "row")),
            P(("grp", "row"), None),
            P(("grp", "row"), None, None, None),
            P(),
            P(),
        ),
        out_specs=(P(("grp", "row"), None), P(("grp", "row"), None), P()),
        check_vma=False,
    )
```

```python
import functools

import jax
import jax.numpy as jnp
from jax import lax
from jax.experimental import pallas as pl
from jax.experimental.pallas import tpu as pltpu
from jax.sharding import PartitionSpec as P

MESH = pl.DeviceIdType.MESH
BF16 = jnp.bfloat16
F32 = jnp.float32
CORES = 2
CHUNKS = 4


def matmul(left, right):
    return jnp.dot(left, right, preferred_element_type=F32)


def matmul_nt(left, right):
    return lax.dot_general(left, right, (((1,), (1,)), ((), ())), preferred_element_type=F32)


def layer_kernel(
    side, depth, scale,
    cols_in, feat, cot, deg, vals, w_self, w_neigh,
    out, fgrad, wgrad,
    cols, places_v, places, feats_all, hidden_all, adj, vals_v, cot_v, deg_v, ws_v, wn_v,
    inv, acc, base, left, gp, out_v, fg_v,
    pair_out, pair_in, keep, s1, r1, r2, r3, r5,
    in_sem, out_sem, ring, near, sib, ag_send, ar_send, ar_recv, relay,
):
    rows, width = gp.shape
    tile = vals_v.shape[2]
    slots = vals_v.shape[1]
    per_dev = rows // tile
    devs = depth * CORES
    half = depth // 2
    rounds = relay.shape[0]
    chunk = rows // CHUNKS
    piece = width // side

    grp, row = lax.axis_index("grp"), lax.axis_index("row")
    gx, gy = lax.div(grp, side), lax.rem(grp, side)
    z, core = lax.div(row, CORES), lax.rem(row, CORES)
    other = 1 - core
    first = (1 - core) * gx + core * gy
    second = (1 - core) * gy + core * gx

    def on_first(p):
        return ((1 - core) * (p * side + gy) + core * (gx * side + p), row)

    def on_second(p):
        return ((1 - core) * (gx * side + p) + core * (p * side + gy), row)

    def on_z(p):
        return (grp, p * CORES + core)

    sibling = (grp, z * CORES + other)

    ins = [
        pltpu.make_async_copy(feat, feats_all.at[row], in_sem.at[0]),
        pltpu.make_async_copy(vals, vals_v, in_sem.at[1]),
        pltpu.make_async_copy(deg, deg_v, in_sem.at[2]),
        pltpu.make_async_copy(w_self, ws_v, in_sem.at[3]),
        pltpu.make_async_copy(w_neigh, wn_v, in_sem.at[4]),
        pltpu.make_async_copy(cot, cot_v, in_sem.at[5]),
        pltpu.make_async_copy(cols_in, cols, in_sem.at[6]),
    ]
    for copy in ins:
        copy.start()

    barrier = pltpu.get_barrier_semaphore()
    up, down = lax.rem(z + 1, depth), lax.rem(z + depth - 1, depth)
    around = [
        on_first(lax.rem(first + 1, side)), on_first(lax.rem(first + side - 1, side)),
        on_second(lax.rem(second + 1, side)), on_second(lax.rem(second + side - 1, side)),
    ]
    for device in [on_z(up), on_z(down), sibling] + around:
        pl.semaphore_signal(barrier, inc=1, device_id=device, device_id_type=MESH)
    pl.semaphore_wait(barrier, 3 + len(around))

    def relay_send(i):
        for device in around:
            pl.semaphore_signal(relay.at[i], inc=1, device_id=device, device_id_type=MESH)

    def relay_wait(i):
        pl.semaphore_wait(relay.at[i], len(around))

    onward = on_z(core * down + other * up)

    def chip(hop):
        return lax.rem(z + (2 * core - 1) * hop + depth, depth)

    def part(buf, hop, own, k):
        who = core if own else other
        return buf.at[chip(hop) * CORES + who, pl.ds(k * chunk, chunk)]

    def ring_copy(buf, which, hop, own, k, src=None):
        ref = part(buf, hop, own, k)
        return pltpu.make_async_remote_copy(
            src_ref=ref if src is None else src, dst_ref=ref, send_sem=ag_send.at[which],
            recv_sem=ring.at[which, 0 if own else 1, hop, k], device_id=onward, device_id_type=MESH)

    def ring_wait(buf, which, hop, own, k):
        ref = part(buf, hop, own, k)
        pltpu.make_async_remote_copy(
            src_ref=ref, dst_ref=ref, send_sem=ag_send.at[which],
            recv_sem=ring.at[which, 0 if own else 1, hop - 1, k],
            device_id=onward, device_id_type=MESH).wait_recv()

    def sib_copy(ref, which, sem, src=None):
        return pltpu.make_async_remote_copy(
            src_ref=ref if src is None else src, dst_ref=ref, send_sem=ag_send.at[which],
            recv_sem=sem, device_id=sibling, device_id_type=MESH)

    def launch_own(buf, which, origin):
        for k in range(CHUNKS):
            src = origin.at[pl.ds(k * chunk, chunk)]
            sib_copy(part(buf, 0, True, k), which, near.at[which, k], src).start()
            ring_copy(buf, which, 0, True, k, src).start()

    def launch_other(buf, which):
        def one(k, _):
            sib_copy(part(buf, 0, False, k), which, near.at[which, k]).wait_recv()
            ring_copy(buf, which, 0, False, k).start()
            return 0
        lax.fori_loop(0, CHUNKS, one, 0)

    def hop_in(buf, which, hop):
        for own in (True, False)[:2 if hop < half else 1]:
            def one(k, _):
                ring_wait(buf, which, hop, own, k)
                if hop < half - 1 or (hop == half - 1 and own):
                    ring_copy(buf, which, hop, own, k).start()
                sib_copy(part(buf, hop, own, k), which, sib.at[which, hop - 1, 0 if own else 1]).start()
                return 0
            lax.fori_loop(0, CHUNKS, one, 0, unroll=True)

    def sib_in(buf, which, hop):
        for i in range(2 if hop < half else 1):
            block = buf.at[0]
            sib_copy(block, which, sib.at[which, hop - 1, i]).wait_recv()

    def sent(buf, which):
        blocks = buf.at[pl.ds(0, 2 * depth - 1)]
        sib_copy(blocks, which, near.at[which, 0]).wait_send()

    def add(buf, hop):
        at = chip(hop)
        acc[...] += matmul(adj[at], buf[pl.ds(CORES * at, CORES)].reshape(CORES * rows, width))

    launch_own(feats_all, 0, feat)
    relay_send(0)
    launch_other(feats_all, 0)

    ins[6].wait()
    lane = lax.broadcasted_iota(jnp.int32, (per_dev, 128), 1)
    place, listed = jnp.zeros_like(lane), jnp.zeros_like(lane)
    for s in range(slots):
        same = cols[:, s:s + 1] == lane
        place = jnp.where(same, s, place)
        listed = jnp.where(same, 1, listed)
    places_v[0:per_dev, :] = place
    places_v[per_dev:2 * per_dev, :] = listed
    to_scalar = pltpu.make_async_copy(places_v, places, in_sem.at[7])
    to_scalar.start()
    ins[1].wait()
    to_scalar.wait()

    def build(hop):
        at = chip(hop)
        for i in range(per_dev):
            for j in range(CORES * per_dev):
                col = at * (CORES * per_dev) + j
                listed = places[per_dev + i, col]
                adj[at, pl.ds(i * tile, tile), pl.ds(j * tile, tile)] = (
                    vals_v[i, places[i, col]] * jnp.float32(listed).astype(BF16))

    build(0)
    for copy in ins[:1] + ins[2:6]:
        copy.wait()
    for i in range(per_dev):
        line = 1.0 / deg_v[pl.ds(i, 1), :].astype(F32)
        square = jnp.transpose(jnp.broadcast_to(line, (tile, tile)))
        for j in range(width // tile):
            inv[pl.ds(i * tile, tile), pl.ds(j * tile, tile)] = square

    left[0] = jnp.transpose(feats_all[row])
    base[...] = matmul(feats_all[row], ws_v[...])
    acc[...] = jnp.zeros_like(acc)
    add(feats_all, 0)
    for hop in range(1, half + 1):
        hop_in(feats_all, 0, hop)
        build(hop)
        if hop < half:
            build(-hop)
            add(feats_all, hop)
        if 1 < hop <= rounds + 1:
            relay_wait(hop - 2)
            if hop <= rounds:
                relay_send(hop - 1)
    for hop in range(1, half + 1):
        sib_in(feats_all, 0, hop)
        add(feats_all, -hop)
    for i in range(half - 1, rounds):
        relay_wait(i)
        if i + 1 < rounds:
            relay_send(i + 1)

    aggregate = (acc[...] * inv[...]).astype(BF16)
    pre = base[...] + matmul(aggregate, wn_v[...])
    left[1] = jnp.transpose(aggregate)
    sig = jax.nn.sigmoid(pre)
    gp[...] = (cot_v[...].astype(F32) * sig * (1.0 + pre * (1.0 - sig))).astype(BF16)
    def far_first(count):
        return sorted(range(1, count), key=lambda i: (-min(i, count - i), i))

    def spread(src, dst, stage, peer, me, count):
        for i in far_first(count):
            p = lax.rem(me + i, count)
            pltpu.make_async_remote_copy(
                src_ref=src(p), dst_ref=dst.at[me], send_sem=ar_send.at[stage],
                recv_sem=ar_recv.at[stage], device_id=peer(p), device_id_type=MESH).start()

    def arrived(dst, stage, count):
        ref = dst.at[pl.ds(0, count - 1)]
        copy = pltpu.make_async_remote_copy(
            src_ref=ref, dst_ref=ref, send_sem=ar_send.at[stage],
            recv_sem=ar_recv.at[stage], device_id=sibling, device_id_type=MESH)
        copy.wait_recv()

    def left_here(dst, stage, count):
        ref = dst.at[pl.ds(0, count - 1)]
        pltpu.make_async_remote_copy(
            src_ref=ref, dst_ref=ref, send_sem=ar_send.at[stage],
            recv_sem=ar_recv.at[stage], device_id=sibling, device_id_type=MESH).wait_send()

    pair = pltpu.make_async_remote_copy(
        src_ref=pair_out, dst_ref=pair_in, send_sem=ar_send.at[0],
        recv_sem=ar_recv.at[0], device_id=sibling, device_id_type=MESH)
    swap = pltpu.make_async_remote_copy(
        src_ref=r5, dst_ref=wgrad.at[core], send_sem=ar_send.at[6],
        recv_sem=ar_recv.at[6], device_id=sibling, device_id_type=MESH)

    write_wg = pltpu.make_async_copy(r5, wgrad.at[core], out_sem.at[2])

    def stage0():
        pair_out[...] = matmul(left[other], gp[...]).astype(BF16)
        pair.start()
        hidden_all[row] = (matmul_nt(gp[...], wn_v[...]) * inv[...]).astype(BF16)
        launch_own(hidden_all, 1, hidden_all.at[row])
        keep[...] = matmul(left[core], gp[...])

    def stage1():
        pair.wait_recv()

        def ready(p):
            part = pl.ds(pl.multiple_of(p * piece, piece), piece)
            s1[p] = (keep[part, :] + pair_in[part, :].astype(F32)).astype(BF16)
            return s1.at[p]

        spread(ready, r1, 1, on_first, first, side)
        r1[first] = ready(first)[...]

    z_early = core if side == depth else 0

    def on_cross(by_z, p):
        across, along = on_second(p), on_z(p)
        return tuple(by_z * a + (1 - by_z) * b for a, b in zip(along, across))

    def total(ref, count):
        value = ref[0].astype(F32)
        for p in range(1, count):
            value += ref[p].astype(F32)
        return value

    def cross(by_z, dst, stage, count, value):
        me = by_z * z + (1 - by_z) * second
        dst[me] = value.astype(BF16)
        spread(lambda p: dst.at[me], dst, stage, functools.partial(on_cross, by_z), me, count)

    def stage2():
        arrived(r1, 1, side)
        cross(z_early, r2, 2, side, total(r1, side))

    def stage3():
        arrived(r2, 2, side)
        cross(1 - z_early, r3, 3, depth, total(r2, side))

    def stage5():
        arrived(r3, 3, depth)
        r5[first] = (total(r3, depth) * scale).astype(BF16)
        spread(lambda p: r5.at[first], r5, 5, on_first, first, side)

    def stage6():
        arrived(r5, 5, side)
        swap.start()
        write_wg.start()

    stage0()
    stage1()
    launch_other(hidden_all, 1)
    out_v[...] = (pre * sig).astype(BF16)
    write_out = pltpu.make_async_copy(out_v, out, out_sem.at[0])
    write_out.start()
    acc[...] = matmul_nt(gp[...], ws_v[...])
    add(hidden_all, 0)
    stages = [stage2, stage3, stage5]
    for hop in range(1, half + 1):
        hop_in(hidden_all, 1, hop)
        if stages:
            stages.pop(0)()
        if hop < half:
            add(hidden_all, hop)
    for stage in stages:
        stage()
    for hop in range(1, half + 1):
        sib_in(hidden_all, 1, hop)
        add(hidden_all, -hop)
    fg_v[...] = acc[...].astype(BF16)
    write_fg = pltpu.make_async_copy(fg_v, fgrad, out_sem.at[1])
    write_fg.start()

    stage6()
    sent(feats_all, 0)
    sent(hidden_all, 1)
    pair.wait_send()
    for buf, stage, count in ((s1, 1, side), (r2, 2, side), (r3, 3, depth), (r5, 5, side)):
        left_here(buf, stage, count)
    swap.wait()
    write_out.wait()
    write_fg.wait()
    write_wg.wait()


def deliver(out_in, fgrad_in, wgrad_in, out, fgrad, wgrad, out_v, fgrad_v, narrow, wide, sem_in, sem_out):
    halves = wgrad.shape[0]
    loads = [pltpu.make_async_copy(wgrad_in.at[i], narrow.at[i], sem_in.at[i]) for i in range(halves)]
    loads.append(pltpu.make_async_copy(out_in, out_v, sem_in.at[halves]))
    loads.append(pltpu.make_async_copy(fgrad_in, fgrad_v, sem_in.at[halves + 1]))
    stores = [pltpu.make_async_copy(wide.at[i], wgrad.at[i], sem_out.at[i]) for i in range(halves)]
    stores.append(pltpu.make_async_copy(out_v, out, sem_out.at[halves]))
    stores.append(pltpu.make_async_copy(fgrad_v, fgrad, sem_out.at[halves + 1]))
    for load in loads:
        load.start()
    for i in range(halves + 2):
        loads[i].wait()
        if i < halves:
            wide[i] = narrow[i].astype(F32).reshape(wide.shape[1:])
        stores[i].start()
    for store in stores:
        store.wait()


def solution(mesh):
    groups, devs = mesh.shape["grp"], mesh.shape["row"]
    depth = devs // CORES
    side = 1
    while side * side < groups:
        side += 1
    half = depth // 2

    def shards(features, cotangent, degrees, tile_cols, tile_vals, w_self, w_neigh):
        rows, width = features.shape
        row_tiles, slots, tile, _ = tile_vals.shape
        scale = float(rows * devs * groups) ** (-0.5)
        piece = width // side
        block = (rows, width)
        dma = pltpu.SemaphoreType.DMA
        any_spec = pl.BlockSpec(memory_space=pl.ANY)
        hbm = pl.BlockSpec(memory_space=pltpu.HBM)
        results = pl.pallas_call(
            functools.partial(layer_kernel, side, depth, scale),
            out_shape=(
                jax.ShapeDtypeStruct(block, BF16),
                jax.ShapeDtypeStruct(block, BF16),
                jax.ShapeDtypeStruct((2, side, piece, width), BF16),
            ),
            in_specs=[hbm] * 7,
            out_specs=(any_spec,) * 3,
            scratch_shapes=[
                pltpu.VMEM(tile_cols.shape, jnp.int32),
                pltpu.VMEM((2 * row_tiles, 128), jnp.int32),
                pltpu.SMEM((2 * row_tiles, 128), jnp.int32),
                pltpu.VMEM((devs,) + block, BF16),
                pltpu.VMEM((devs,) + block, BF16),
                pltpu.VMEM((depth, rows, CORES * rows), BF16),
                pltpu.VMEM(tile_vals.shape, BF16),
                pltpu.VMEM(block, BF16),
                pltpu.VMEM((row_tiles, tile), jnp.int32),
                pltpu.VMEM((width, width), BF16),
                pltpu.VMEM((width, width), BF16),
                pltpu.VMEM(block, F32),
                pltpu.VMEM(block, F32),
                pltpu.VMEM(block, F32),
                pltpu.VMEM((2, width, rows), BF16),
                pltpu.VMEM(block, BF16),
                pltpu.VMEM(block, BF16),
                pltpu.VMEM(block, BF16),
                pltpu.VMEM((width, width), BF16),
                pltpu.VMEM((width, width), BF16),
                pltpu.VMEM((width, width), F32),
                pltpu.VMEM((side, piece, width), BF16),
                pltpu.VMEM((side, piece, width), BF16),
                pltpu.VMEM((side, piece, width), BF16),
                pltpu.VMEM((depth, piece, width), BF16),
                pltpu.VMEM((side, piece, width), BF16),
                dma((8,)),
                dma((3,)),
                dma((2, 2, half, CHUNKS)),
                dma((2, CHUNKS)),
                dma((2, half, 2)),
                dma((2,)),
                dma((7,)),
                dma((7,)),
                pltpu.SemaphoreType.REGULAR((max(1, side // 2 - 1),)),
            ],
            compiler_params=pltpu.CompilerParams(
                collective_id=0, has_side_effects=True, vmem_limit_bytes=56 * 1024 * 1024),
        )(
            tile_cols, features, cotangent, degrees.reshape(row_tiles, tile), tile_vals, w_self, w_neigh)
        return pl.pallas_call(
            deliver,
            out_shape=(
                jax.ShapeDtypeStruct(block, BF16),
                jax.ShapeDtypeStruct(block, BF16),
                jax.ShapeDtypeStruct((2, width, width), F32),
            ),
            in_specs=[any_spec] * 3,
            out_specs=(any_spec,) * 3,
            scratch_shapes=[
                pltpu.VMEM(block, BF16),
                pltpu.VMEM(block, BF16),
                pltpu.VMEM((2, side, piece, width), BF16),
                pltpu.VMEM((2, width, width), F32),
                dma((4,)),
                dma((4,)),
            ],
            compiler_params=pltpu.CompilerParams(vmem_limit_bytes=56 * 1024 * 1024),
        )(*results)

    return jax.shard_map(
        shards,
        mesh=mesh,
        in_specs=(
            P(("grp", "row"), None),
            P(("grp", "row"), None),
            P(("grp", "row")),
            P(("grp", "row"), None),
            P(("grp", "row"), None, None, None),
            P(),
            P(),
        ),
        out_specs=(P(("grp", "row"), None), P(("grp", "row"), None), P()),
        check_vma=False,
    )
```
